32 devices in a mesh: grp: 2 (over x), gx: 8 (over z, y), gy: 2 (over core).
Axes of the slice: x: 2, y: 2, z: 4, core: 2. Of those that a mesh axis runs over, the one named last changes fastest.
Arguments:
- inputs: bfloat16 [1536, 4096], P(('grp', 'gy'), 'gx'), parts along dimension 0, may hold values from -6 to 6
- out_grad: bfloat16 [1536, 4096], P(('grp', 'gy'), 'gx'), parts along dimension 0, may hold values from -3 to 3
- w_gate: bfloat16 [4096, 14336], P('gy', 'gx'), may hold values from -0.125 to 0.125
- w_up: bfloat16 [4096, 14336], P('gy', 'gx'), may hold values from -0.09375 to 0.09375
- w_down: bfloat16 [14336, 4096], P('gx', 'gy'), may hold values from -0.046875 to 0.046875
Outputs:
- in_grad: bfloat16 [1536, 4096], P(('grp', 'gy'), 'gx'), parts along dimension 0
- gate_grad: bfloat16 [8192, 14336], P(('grp', 'gy'), 'gx'), parts along dimension 0
- up_grad: bfloat16 [8192, 14336], P(('grp', 'gy'), 'gx'), parts along dimension 0
- down_grad: bfloat16 [28672, 4096], P(('grp', 'gx'), 'gy'), parts along dimension 0
The draws below stay inside these ranges and needn't reach their ends.
There are 2 independent parts, one for each index of `grp`. The reference program is written for one: setup_inputs(seed, part) draws one part's arguments, and reference() takes and returns one part's arrays. A program takes and returns all parts, laid end to end along the dimension named above; an argument that names none is the same for every part. Nothing has to cross between parts.
All inputs are finite; a program needn't handle non-finite values.
Results may differ from the reference program's by a relative error of at most 0.0059.
Values may be sent and summed in bfloat16 or wider, within the bound.
A program may use at most 256 MiB of HBM per device.

```python
import jax
import jax.numpy as jnp
from jax import lax

D = 4096
FF = 14336
TOK = 768
N_GY = 2


def spiked(values, key, source, target, parts, factor):
    def block_of(position):
        return (jnp.arange(values.shape[position]) // (values.shape[position] // parts)).reshape((-1,) + (1,) * (values.ndim - 1 - position))

    near = jax.random.permutation(key, parts)[block_of(target)]
    second = (block_of(target) + parts // 2) % parts
    return jnp.where((block_of(source) == near) | (block_of(source) == second), factor * values, values)


def block_scale(key, extent, cuts, smallest, largest):
    def one(dim, parts):
        steps = jax.random.uniform(jax.random.fold_in(jax.random.fold_in(key, 6), dim), (parts,), jnp.float32, smallest / len(cuts), largest / len(cuts))
        return jnp.repeat(jnp.exp(steps), extent[dim] // parts).reshape((-1,) + (1,) * (len(extent) - dim - 1))

    loudness = one(*cuts[0])
    for cut in cuts[1:]:
        loudness = loudness * one(*cut)
    return loudness


def normal_values(own_key, dims, deviation, limit, shards=(), held_as=jnp.bfloat16):
    array = deviation * jax.random.normal(own_key, dims, jnp.float32)
    if shards:
        array = array * block_scale(own_key, dims, shards, -0.22, 0.18)
    return jnp.clip(array, -limit, limit).astype(held_as)


def noise_with(own_key, extent, width, bound, split, heavy, dtype=jnp.bfloat16):
    array = width * jax.random.normal(own_key, extent, jnp.float32)
    if split:
        array = array * block_scale(own_key, extent, split, -0.22, 0.18)
    return jnp.clip(spiked(array, jax.random.fold_in(own_key, 3), *heavy), -bound, bound).astype(dtype)


def setup_inputs(seed: int = 0, part: int = 0) -> dict:
    arg_keys = jax.random.split(jax.random.key(seed), 6)
    part_splits = jax.random.split(jax.random.fold_in(arg_keys[5], part), 6)
    return {
        "inputs": normal_values(part_splits[0], (TOK, D), 1.0, 6.0, ((0, 2), (1, 8))),
        "out_grad": normal_values(part_splits[1], (TOK, D), 0.5, 3.0, ((0, 2), (1, 8))),
        "w_gate": noise_with(arg_keys[2], (D, FF), D ** -0.5, 0.125, ((0, 2), (1, 8)), (1, 0, 8, 2.0)),
        "w_up": normal_values(arg_keys[3], (D, FF), D ** -0.5, 0.09375, ((0, 2), (1, 8))),
        "w_down": normal_values(arg_keys[4], (FF, D), FF ** -0.5, 0.046875, ((0, 8), (1, 2))),
    }


def block_sum(left, right):
    rows = left.shape[0] // N_GY
    left_blocks = left.reshape(N_GY, rows, left.shape[1]).astype(jnp.float32)
    right_blocks = right.reshape(N_GY, rows, right.shape[1]).astype(jnp.float32)
    partials = jnp.einsum("btc,btf->bcf", left_blocks, right_blocks).astype(jnp.bfloat16)
    partials = lax.optimization_barrier(partials)
    return jnp.sum(partials.astype(jnp.float32), axis=0).astype(jnp.bfloat16)


def reference(inputs, out_grad, w_gate, w_up, w_down):
    gate = jnp.dot(inputs, w_gate, preferred_element_type=jnp.float32)
    up = jnp.dot(inputs, w_up, preferred_element_type=jnp.float32)
    sig = jax.nn.sigmoid(gate)
    act = gate * sig
    hidden = (act * up).astype(jnp.bfloat16)
    hidden_grad = jnp.dot(out_grad, w_down.T, preferred_element_type=jnp.float32)
    up_term = (hidden_grad * act).astype(jnp.bfloat16)
    gate_term = (hidden_grad * up * sig * (1.0 + gate * (1.0 - sig))).astype(jnp.bfloat16)
    in_grad = jnp.dot(gate_term, w_gate.T, preferred_element_type=jnp.float32)
    in_grad = in_grad + jnp.dot(up_term, w_up.T, preferred_element_type=jnp.float32)
    gate_grad = block_sum(inputs, gate_term)
    up_grad = block_sum(inputs, up_term)
    down_grad = block_sum(hidden, out_grad)
    return (in_grad.astype(jnp.bfloat16), gate_grad, up_grad, down_grad)
```

```python
import functools

import jax
import jax.numpy as jnp
from jax import lax
from jax.experimental import pallas as pl
from jax.experimental.pallas import tpu as pltpu
from jax.sharding import PartitionSpec as P

MESH = pl.DeviceIdType.MESH
F32 = jnp.float32
BF16 = jnp.bfloat16


def ring_place(n, me):
    if n > 8:
        return me
    up, side = me // 2, me % 2
    return (1 - side) * up + side * (n - 1 - up)


def ring_member(n, place):
    if n > 8:
        return place
    late = place // (n // 2)
    return (1 - late) * 2 * place + late * (2 * (n - 1 - place) + 1)


def terms_kernel(n, tiles, width, x_in, g_in, wg, wu, wd, hid, gt, ut, x_out, g_out,
                 xb, gb, wgu, wdb, a_own, a_got, b_own, b_got,
                 in_sem, wgu_sem, wd_sem, ring_send, ring_recv, sib_send, sib_recv,
                 part_send, part_recv, out_sem, credit):
    half = n // 2
    me, t = lax.axis_index("gx"), lax.axis_index("gy")
    sib = 1 - t
    place = ring_place(n, me)
    right = ring_member(n, lax.rem(place + 1, n))
    left = ring_member(n, lax.rem(place + n - 1, n))
    dl = xb.shape[-1]
    rows = 4 * xb.shape[-2]

    def own_in(arr, c):
        src, buf = ((x_in, xb), (g_in, gb))[arr]
        return pltpu.make_async_copy(src.at[c], buf.at[me, t, c], in_sem.at[arr, c])

    for arr in range(2):
        for c in range(2):
            own_in(arr, c).start()

    barrier = pltpu.get_barrier_semaphore()
    pl.semaphore_signal(barrier, inc=1, device_id={"gx": left}, device_id_type=MESH)
    pl.semaphore_signal(barrier, inc=1, device_id={"gx": right}, device_id_type=MESH)
    pl.semaphore_signal(barrier, inc=1, device_id={"gy": sib}, device_id_type=MESH)
    pl.semaphore_wait(barrier, 3)

    def hop(arr, j, s, c, way):
        buf = (xb, gb)[arr]
        return pltpu.make_async_remote_copy(
            src_ref=buf.at[j, t, c], dst_ref=buf.at[j, t, c],
            send_sem=ring_send.at[arr, s - 1, c, way], recv_sem=ring_recv.at[arr, s - 1, c, way],
            device_id={"gx": (right, left)[way]}, device_id_type=MESH)

    def across(arr, j, c, whose):
        buf = (xb, gb)[arr]
        return pltpu.make_async_remote_copy(
            src_ref=buf.at[j, whose, c], dst_ref=buf.at[j, whose, c],
            send_sem=sib_send.at[arr, j % half, c], recv_sem=sib_recv.at[arr, j % half, c],
            device_id={"gy": sib}, device_id_type=MESH)

    def to_sibling(arr, j, c):
        @pl.when(j // half != t)
        def _():
            across(arr, j, c, t).start()

    def source(s, way):
        return ring_member(n, lax.rem(place + n + (s if way else -s), n))

    def begin(arr):
        for c in range(2):
            own_in(arr, c).wait()
            for way in range(2):
                hop(arr, me, 1, c, way).start()
            to_sibling(arr, me, c)

    def event(arr, e):
        s, c = 1 + e // 2, e % 2
        for way in range(2):
            j = source(s, way)
            hop(arr, j, s, c, way).wait_recv()

            @pl.when((s + 1 < half) | (c == way))
            def _():
                hop(arr, j, s + 1, c, way).start()

            to_sibling(arr, j, c)

    def last_event(arr):
        for way in range(2):
            j = source(half, way)
            hop(arr, j, half, way, way).wait_recv()
            to_sibling(arr, j, way)

    def from_sibling(arr):
        def one(k, carry):
            for c in range(2):
                across(arr, t * half + k, c, sib).wait_recv()
            return carry
        lax.fori_loop(0, half, one, 0)

    def weights(i, which):
        return pltpu.make_async_copy(
            (wg, wu)[which].at[:, pl.ds(pl.multiple_of(i * width, 128), width)],
            wgu.at[i % 2, which], wgu_sem.at[i % 2, which])

    def down(i):
        return pltpu.make_async_copy(
            wd.at[pl.ds(pl.multiple_of(i * width, 16), width), :], wdb.at[i], wd_sem.at[i])

    def part(which, i):
        src, dst = ((a_own, a_got), (b_own, b_got), (a_got, b_got))[which]
        return pltpu.make_async_remote_copy(
            src_ref=src.at[i], dst_ref=dst.at[i],
            send_sem=part_send.at[which, i], recv_sem=part_recv.at[which, i],
            device_id={"gy": sib}, device_id_type=MESH)

    begin(0)
    for i in range(min(2, tiles)):
        weights(i, 0).start()
        weights(i, 1).start()
    for i in range(tiles):
        down(i).start()

    def x_step(e, carry):
        event(0, e)
        return carry
    lax.fori_loop(0, 2 * (half - 1), x_step, 0)
    begin(1)
    last_event(0)
    from_sibling(0)

    def first_half(i):
        at = pl.ds(pl.multiple_of(i * width, 128), width)
        part(0, i).wait()
        part(1, i).wait()
        gate = a_own[i] + a_got[i]
        up = b_own[i] + b_got[i]
        sig = 1.0 / (1.0 + jnp.exp(-gate))
        act = gate * sig
        hid[:, at] = (act * up).astype(BF16)
        a_own[i] = act
        b_own[i] = up * sig * (1.0 + gate * (1.0 - sig))

    def tile(i):
        for which, own in ((0, a_own), (1, b_own)):
            weights(i, which).wait()
            total = None
            for k in range(half):
                lhs = xb[t * half + k].reshape(rows, dl)
                term = jnp.dot(lhs, wgu[i % 2, which, k * dl:(k + 1) * dl, :], preferred_element_type=F32)
                total = term if total is None else total + term
            own[i] = total
            part(which, i).start()

            @pl.when(i + 2 < tiles)
            def _():
                weights(i + 2, which).start()

        @pl.when(i > 0)
        def _():
            first_half(i - 1)

    def g_step(e, carry):
        event(1, e)

        @pl.when(e < tiles)
        def _():
            tile(e)
        return carry
    lax.fori_loop(0, 2 * (half - 1), g_step, 0)
    last_event(1)

    def rest(i, carry):
        tile(i)
        return carry
    lax.fori_loop(min(2 * (half - 1), tiles), tiles, rest, 0)
    first_half(tiles - 1)
    pl.semaphore_signal(credit, inc=1, device_id={"gy": sib}, device_id_type=MESH)
    from_sibling(1)

    def outs(arr, k):
        buf, out = ((xb, x_out), (gb, g_out))[arr]
        return pltpu.make_async_copy(
            buf.at[t * half + k], out.at[:, :, :, pl.ds(k * dl, dl)], out_sem.at[arr, k])

    for arr in range(2):
        for k in range(half):
            outs(arr, k).start()
    pl.semaphore_wait(credit, 1)

    def second_half(i):
        at = pl.ds(pl.multiple_of(i * width, 128), width)
        part(2, i).wait_recv()
        grad = a_got[i] + b_got[i]
        ut[:, at] = (grad * a_own[i]).astype(BF16)
        gt[:, at] = (grad * b_own[i]).astype(BF16)

    def grad_tile(i, carry):
        down(i).wait()
        total = None
        for k in range(half):
            lhs = gb[t * half + k].reshape(rows, dl)
            term = lax.dot_general(lhs, wdb[i, :, k * dl:(k + 1) * dl], (((1,), (1,)), ((), ())),
                                   preferred_element_type=F32)
            total = term if total is None else total + term
        a_got[i] = total
        part(2, i).start()

        @pl.when(i > 0)
        def _():
            second_half(i - 1)
        return carry
    lax.fori_loop(0, tiles, grad_tile, 0)
    second_half(tiles - 1)

    def sent(i, carry):
        part(2, i).wait_send()
        return carry
    lax.fori_loop(0, tiles, sent, 0)

    for arr in range(2):
        for k in range(half):
            outs(arr, k).wait()

        def crossed(k, carry):
            for c in range(2):
                across(arr, sib * half + k, c, t).wait_send()
            return carry
        lax.fori_loop(0, half, crossed, 0)

        def hopped(s, carry):
            for c in range(2):
                for way in range(2):
                    hop(arr, me, s, c, way).wait_send()
            return carry
        lax.fori_loop(1, half, hopped, 0)
        for way in range(2):
            hop(arr, me, half, way, way).wait_send()


def terms(n, inputs, out_grad, w_gate, w_up, w_down):
    tok, dl = inputs.shape
    dh, ff = w_gate.shape
    half = n // 2
    width = 256 if ff % 256 == 0 else ff
    tiles = ff // width
    anyspace = pl.BlockSpec(memory_space=pl.ANY)
    vmem = pl.BlockSpec(memory_space=pltpu.VMEM)
    quarter = tok // 2
    term = jax.ShapeDtypeStruct((2 * tok, ff), BF16)
    gathered = jax.ShapeDtypeStruct((2, 2, quarter, dh), BF16)
    dma = pltpu.SemaphoreType.DMA
    return pl.pallas_call(
        functools.partial(terms_kernel, n, tiles, width),
        out_shape=(term, term, term, gathered, gathered),
        in_specs=[anyspace] * 5,
        out_specs=(vmem, vmem, vmem, anyspace, anyspace),
        scratch_shapes=[
            pltpu.VMEM((n, 2, 2, quarter, dl), BF16),
            pltpu.VMEM((n, 2, 2, quarter, dl), BF16),
            pltpu.VMEM((2, 2, dh, width), BF16),
            pltpu.VMEM((tiles, width, dh), BF16),
            pltpu.VMEM((tiles, 2 * tok, width), F32),
            pltpu.VMEM((tiles, 2 * tok, width), F32),
            pltpu.VMEM((tiles, 2 * tok, width), F32),
            pltpu.VMEM((tiles, 2 * tok, width), F32),
            dma((2, 2)),
            dma((2, 2)),
            dma((tiles,)),
            dma((2, half, 2, 2)),
            dma((2, half, 2, 2)),
            dma((2, half, 2)),
            dma((2, half, 2)),
            dma((3, tiles)),
            dma((3, tiles)),
            dma((2, half)),
            pltpu.SemaphoreType.REGULAR,
        ],
        compiler_params=pltpu.CompilerParams(
            collective_id=0, has_side_effects=True, vmem_limit_bytes=62 * 1024 * 1024),
        cost_estimate=pl.CostEstimate(
            flops=12 * tok * dh * ff, bytes_accessed=10 * dh * ff, transcendentals=2 * tok * ff),
    )(inputs.reshape(2, quarter, dl), out_grad.reshape(2, quarter, dl), w_gate, w_up, w_down)


def reduce_ring(n, blocks, me):
    half = n // 2
    members = [int(ring_member(n, p)) for p in range(n)]
    ways = [
        [(members[p], members[(p + 1) % n]) for p in range(n)],
        [(members[p], members[(p - 1) % n]) for p in range(n)],
    ]
    place = ring_place(n, me)
    got = [None, None]
    for s in range(half):
        for way in range(2):
            d = half - s
            block = blocks(ring_member(n, (place + n + (-d if way else d)) % n))
            rows = block.shape[0]
            if s == 0:
                block = block[way * rows // 2:(way + 1) * rows // 2]
            elif s == 1:
                pad = (0, rows // 2) if way == 0 else (rows // 2, 0)
                block = block + jnp.pad(got[way].astype(F32), (pad, (0, 0)))
            else:
                block = block + got[way].astype(F32)
            got[way] = lax.ppermute(block.astype(BF16), "gx", ways[way])
    return (blocks(me) + got[0].astype(F32) + got[1].astype(F32)).astype(BF16)


def on_device(n, inputs, out_grad, w_gate, w_up, w_down):
    tok, dl = inputs.shape
    dh, ff = w_gate.shape
    half = n // 2
    me, t = lax.axis_index("gx"), lax.axis_index("gy")
    hid, gt, ut, xh, gh = terms(n, inputs, out_grad, w_gate, w_up, w_down)
    xh, gh = xh.reshape(2 * tok, dh), gh.reshape(2 * tok, dh)

    def back(rows):
        a = lax.dynamic_slice_in_dim(gt, rows * tok, tok, 0)
        b = lax.dynamic_slice_in_dim(ut, rows * tok, tok, 0)
        nt = (((1,), (1,)), ((), ()))
        return lax.dot_general(a, w_gate, nt, preferred_element_type=F32) + lax.dot_general(
            b, w_up, nt, preferred_element_type=F32)

    theirs = lax.ppermute(back(1 - t).astype(BF16), "gy", [(0, 1), (1, 0)])
    mine = back(t)

    def blocks(q):
        at = (q % half) * dl
        own = lax.dynamic_slice_in_dim(mine, at, dl, 1)
        other = lax.dynamic_slice_in_dim(theirs, at, dl, 1).astype(F32)
        return jnp.where(q // half == t, own, other)

    in_grad = reduce_ring(n, blocks, me)
    tn = (((0,), (0,)), ((), ()))
    gate_grad = lax.dot_general(xh, gt, tn, preferred_element_type=F32).astype(BF16)
    up_grad = lax.dot_general(xh, ut, tn, preferred_element_type=F32).astype(BF16)
    down_grad = lax.dot_general(hid, gh, tn, preferred_element_type=F32).astype(BF16)
    return in_grad, gate_grad, up_grad, down_grad


def solution(mesh):
    in_specs = (
        P(("grp", "gy"), "gx"),
        P(("grp", "gy"), "gx"),
        P("gy", "gx"),
        P("gy", "gx"),
        P("gx", "gy"),
    )
    out_specs = (
        P(("grp", "gy"), "gx"),
        P(("grp", "gy"), "gx"),
        P(("grp", "gy"), "gx"),
        P(("grp", "gx"), "gy"),
    )
    return jax.shard_map(
        functools.partial(on_device, mesh.shape["gx"]),
        mesh=mesh, in_specs=in_specs, out_specs=out_specs, check_vma=False
    )
```

```python
import functools

import jax
import jax.numpy as jnp
from jax import lax
from jax.experimental import pallas as pl
from jax.experimental.pallas import tpu as pltpu
from jax.sharding import PartitionSpec as P

MESH = pl.DeviceIdType.MESH
F32 = jnp.float32
BF16 = jnp.bfloat16


def ring_place(n, me):
    if n > 8:
        return me
    up, side = me // 2, me % 2
    return (1 - side) * up + side * (n - 1 - up)


def ring_member(n, place):
    if n > 8:
        return place
    late = place // (n // 2)
    return (1 - late) * 2 * place + late * (2 * (n - 1 - place) + 1)


def terms_kernel(n, tiles, width, x_in, g_in, wg, wu, wd, hid, gt, ut, x_out, g_out,
                 xb, gb, wgu, wdb, a_own, a_got, b_own, b_got,
                 in_sem, wgu_sem, wd_sem, ring_send, ring_recv, sib_send, sib_recv,
                 part_send, part_recv, out_sem, credit):
    half = n // 2
    me, t = lax.axis_index("gx"), lax.axis_index("gy")
    sib = 1 - t
    place = ring_place(n, me)
    right = ring_member(n, lax.rem(place + 1, n))
    left = ring_member(n, lax.rem(place + n - 1, n))
    dl, dh = x_in.shape[-1], x_out.shape[-1]
    rows = 4 * xb.shape[-2]
    my_half = pl.ds(pl.multiple_of(t * dh, 128), dh)

    def cell(buf, j, whose, c):
        return buf.at[whose, c, :, pl.ds(pl.multiple_of(j * dl, 128), dl)]

    def own_in(arr, c):
        src, buf = ((x_in, xb), (g_in, gb))[arr]
        return pltpu.make_async_copy(src.at[c], cell(buf, me, t, c), in_sem.at[arr, c])

    for arr in range(2):
        for c in range(2):
            own_in(arr, c).start()

    barrier = pltpu.get_barrier_semaphore()
    pl.semaphore_signal(barrier, inc=1, device_id={"gx": left}, device_id_type=MESH)
    pl.semaphore_signal(barrier, inc=1, device_id={"gx": right}, device_id_type=MESH)
    pl.semaphore_signal(barrier, inc=1, device_id={"gy": sib}, device_id_type=MESH)
    pl.semaphore_wait(barrier, 3)

    def hop(arr, j, s, c, way):
        buf = (xb, gb)[arr]
        return pltpu.make_async_remote_copy(
            src_ref=cell(buf, j, t, c), dst_ref=cell(buf, j, t, c),
            send_sem=ring_send.at[arr, s - 1, c, way], recv_sem=ring_recv.at[arr, s - 1, c, way],
            device_id={"gx": (right, left)[way]}, device_id_type=MESH)

    def across(arr, j, c, whose):
        buf = (xb, gb)[arr]
        return pltpu.make_async_remote_copy(
            src_ref=cell(buf, j, whose, c), dst_ref=cell(buf, j, whose, c),
            send_sem=sib_send.at[arr, j % half, c], recv_sem=sib_recv.at[arr, j % half, c],
            device_id={"gy": sib}, device_id_type=MESH)

    def to_sibling(arr, j, c):
        @pl.when(j // half != t)
        def _():
            across(arr, j, c, t).start()

    def source(s, way):
        return ring_member(n, lax.rem(place + n + (s if way else -s), n))

    def begin(arr):
        for c in range(2):
            own_in(arr, c).wait()
            for way in range(2):
                hop(arr, me, 1, c, way).start()
            to_sibling(arr, me, c)

    def event(arr, e):
        s, c = 1 + e // 2, e % 2
        for way in range(2):
            j = source(s, way)
            hop(arr, j, s, c, way).wait_recv()

            @pl.when((s + 1 < half) | (c == way))
            def _():
                hop(arr, j, s + 1, c, way).start()

            to_sibling(arr, j, c)

    def last_event(arr):
        for way in range(2):
            j = source(half, way)
            hop(arr, j, half, way, way).wait_recv()
            to_sibling(arr, j, way)

    def from_sibling(arr):
        def one(k, carry):
            for c in range(2):
                across(arr, t * half + k, c, sib).wait_recv()
            return carry
        lax.fori_loop(0, half, one, 0)

    def weights(i, which):
        return pltpu.make_async_copy(
            (wg, wu)[which].at[:, pl.ds(pl.multiple_of(i * width, 128), width)],
            wgu.at[i % 2, which], wgu_sem.at[i % 2, which])

    def down(i):
        return pltpu.make_async_copy(
            wd.at[pl.ds(pl.multiple_of(i * width, 16), width), :], wdb.at[i], wd_sem.at[i])

    def part(which, i):
        src, dst = ((a_own, a_got), (b_own, b_got), (a_got, b_got))[which]
        return pltpu.make_async_remote_copy(
            src_ref=src.at[i], dst_ref=dst.at[i],
            send_sem=part_send.at[which, i], recv_sem=part_recv.at[which, i],
            device_id={"gy": sib}, device_id_type=MESH)

    begin(0)
    for i in range(min(2, tiles)):
        weights(i, 0).start()
        weights(i, 1).start()
    for i in range(tiles):
        down(i).start()

    def x_step(e, carry):
        event(0, e)
        return carry
    lax.fori_loop(0, 2 * (half - 1), x_step, 0)
    begin(1)
    last_event(0)
    from_sibling(0)

    def first_half(i):
        at = pl.ds(pl.multiple_of(i * width, 128), width)
        part(0, i).wait()
        part(1, i).wait()
        gate = a_own[i] + a_got[i]
        up = b_own[i] + b_got[i]
        sig = 1.0 / (1.0 + jnp.exp(-gate))
        act = gate * sig
        hid[:, at] = (act * up).astype(BF16)
        a_own[i] = act
        b_own[i] = up * sig * (1.0 + gate * (1.0 - sig))

    def tile(i):
        for which, own in ((0, a_own), (1, b_own)):
            weights(i, which).wait()
            lhs = xb[:, :, :, my_half].reshape(rows, dh)
            own[i] = jnp.dot(lhs, wgu[i % 2, which], preferred_element_type=F32)
            part(which, i).start()

            @pl.when(i + 2 < tiles)
            def _():
                weights(i + 2, which).start()

        @pl.when(i > 0)
        def _():
            first_half(i - 1)

    def g_step(e, carry):
        event(1, e)

        @pl.when(e < tiles)
        def _():
            tile(e)
        return carry
    lax.fori_loop(0, 2 * (half - 1), g_step, 0)
    last_event(1)

    def rest(i, carry):
        tile(i)
        return carry
    lax.fori_loop(min(2 * (half - 1), tiles), tiles, rest, 0)
    first_half(tiles - 1)
    pl.semaphore_signal(credit, inc=1, device_id={"gy": sib}, device_id_type=MESH)
    from_sibling(1)

    def outs(arr):
        buf, out = ((xb, x_out), (gb, g_out))[arr]
        return pltpu.make_async_copy(buf.at[:, :, :, my_half], out, out_sem.at[arr])

    for arr in range(2):
        outs(arr).start()
    pl.semaphore_wait(credit, 1)

    def second_half(i):
        at = pl.ds(pl.multiple_of(i * width, 128), width)
        part(2, i).wait_recv()
        grad = a_got[i] + b_got[i]
        ut[:, at] = (grad * a_own[i]).astype(BF16)
        gt[:, at] = (grad * b_own[i]).astype(BF16)

    def grad_tile(i, carry):
        down(i).wait()
        lhs = gb[:, :, :, my_half].reshape(rows, dh)
        a_got[i] = lax.dot_general(lhs, wdb[i], (((1,), (1,)), ((), ())), preferred_element_type=F32)
        part(2, i).start()

        @pl.when(i > 0)
        def _():
            second_half(i - 1)
        return carry
    lax.fori_loop(0, tiles, grad_tile, 0)
    second_half(tiles - 1)

    def sent(i, carry):
        part(2, i).wait_send()
        return carry
    lax.fori_loop(0, tiles, sent, 0)

    for arr in range(2):
        outs(arr).wait()

        def crossed(k, carry):
            for c in range(2):
                across(arr, sib * half + k, c, t).wait_send()
            return carry
        lax.fori_loop(0, half, crossed, 0)

        def hopped(s, carry):
            for c in range(2):
                for way in range(2):
                    hop(arr, me, s, c, way).wait_send()
            return carry
        lax.fori_loop(1, half, hopped, 0)
        for way in range(2):
            hop(arr, me, half, way, way).wait_send()


def terms(n, inputs, out_grad, w_gate, w_up, w_down):
    tok, dl = inputs.shape
    dh, ff = w_gate.shape
    half = n // 2
    width = 256 if ff % 256 == 0 else ff
    tiles = ff // width
    anyspace = pl.BlockSpec(memory_space=pl.ANY)
    vmem = pl.BlockSpec(memory_space=pltpu.VMEM)
    quarter = tok // 2
    term = jax.ShapeDtypeStruct((2 * tok, ff), BF16)
    gathered = jax.ShapeDtypeStruct((2, 2, quarter, dh), BF16)
    dma = pltpu.SemaphoreType.DMA
    return pl.pallas_call(
        functools.partial(terms_kernel, n, tiles, width),
        out_shape=(term, term, term, gathered, gathered),
        in_specs=[anyspace] * 5,
        out_specs=(vmem, vmem, vmem, anyspace, anyspace),
        scratch_shapes=[
            pltpu.VMEM((2, 2, quarter, n * dl), BF16),
            pltpu.VMEM((2, 2, quarter, n * dl), BF16),
            pltpu.VMEM((2, 2, dh, width), BF16),
            pltpu.VMEM((tiles, width, dh), BF16),
            pltpu.VMEM((tiles, 2 * tok, width), F32),
            pltpu.VMEM((tiles, 2 * tok, width), F32),
            pltpu.VMEM((tiles, 2 * tok, width), F32),
            pltpu.VMEM((tiles, 2 * tok, width), F32),
            dma((2, 2)),
            dma((2, 2)),
            dma((tiles,)),
            dma((2, half, 2, 2)),
            dma((2, half, 2, 2)),
            dma((2, half, 2)),
            dma((2, half, 2)),
            dma((3, tiles)),
            dma((3, tiles)),
            dma((2,)),
            pltpu.SemaphoreType.REGULAR,
        ],
        compiler_params=pltpu.CompilerParams(
            collective_id=0, has_side_effects=True, vmem_limit_bytes=62 * 1024 * 1024),
        cost_estimate=pl.CostEstimate(
            flops=12 * tok * dh * ff, bytes_accessed=10 * dh * ff, transcendentals=2 * tok * ff),
    )(inputs.reshape(2, quarter, dl), out_grad.reshape(2, quarter, dl), w_gate, w_up, w_down)


def reduce_ring(n, blocks, me, work):
    half = n // 2
    members = [int(ring_member(n, p)) for p in range(n)]
    ways = [
        [(members[p], members[(p + 1) % n]) for p in range(n)],
        [(members[p], members[(p - 1) % n]) for p in range(n)],
    ]
    place = ring_place(n, me)
    got = [None, None]
    at_step = {(i + 1) * half // (len(work) + 1): i for i in range(len(work))}
    made = []
    for s in range(half):
        sends = []
        for way in range(2):
            d = half - s
            block = blocks(ring_member(n, (place + n + (-d if way else d)) % n))
            rows = block.shape[0]
            if s == 0:
                block = block[way * rows // 2:(way + 1) * rows // 2]
            elif s == 1:
                pad = (0, rows // 2) if way == 0 else (rows // 2, 0)
                block = block + jnp.pad(got[way].astype(F32), (pad, (0, 0)))
            else:
                block = block + got[way].astype(F32)
            sends.append(block.astype(BF16))
        if s in at_step:
            function, operand = work[at_step[s]]
            sends[0], sends[1], operand = lax.optimization_barrier((sends[0], sends[1], operand))
            product = function(operand)
        got = [lax.ppermute(sends[way], "gx", ways[way]) for way in range(2)]
        if s in at_step:
            got[0], got[1], product = lax.optimization_barrier((got[0], got[1], product))
            made.append(product)
    total = (blocks(me) + got[0].astype(F32) + got[1].astype(F32)).astype(BF16)
    return total, made


def on_device(n, inputs, out_grad, w_gate, w_up, w_down):
    tok, dl = inputs.shape
    dh, ff = w_gate.shape
    half = n // 2
    me, t = lax.axis_index("gx"), lax.axis_index("gy")
    hid, gt, ut, xh, gh = terms(n, inputs, out_grad, w_gate, w_up, w_down)
    xh, gh = xh.reshape(2 * tok, dh), gh.reshape(2 * tok, dh)

    def back(rows):
        a = lax.dynamic_slice_in_dim(gt, rows * tok, tok, 0)
        b = lax.dynamic_slice_in_dim(ut, rows * tok, tok, 0)
        nt = (((1,), (1,)), ((), ()))
        return lax.dot_general(a, w_gate, nt, preferred_element_type=F32) + lax.dot_general(
            b, w_up, nt, preferred_element_type=F32)

    theirs = lax.ppermute(back(1 - t).astype(BF16), "gy", [(0, 1), (1, 0)])
    mine = back(t)

    def blocks(q):
        at = (q % half) * dl
        own = lax.dynamic_slice_in_dim(mine, at, dl, 1)
        other = lax.dynamic_slice_in_dim(theirs, at, dl, 1).astype(F32)
        return jnp.where(q // half == t, own, other)

    def product(left):
        return lambda right: lax.dot_general(
            left, right, (((0,), (0,)), ((), ())), preferred_element_type=F32).astype(BF16)

    in_grad, (gate_grad, up_grad, down_grad) = reduce_ring(
        n, blocks, me, [(product(xh), gt), (product(xh), ut), (product(hid), gh)])
    return in_grad, gate_grad, up_grad, down_grad


def solution(mesh):
    in_specs = (
        P(("grp", "gy"), "gx"),
        P(("grp", "gy"), "gx"),
        P("gy", "gx"),
        P("gy", "gx"),
        P("gx", "gy"),
    )
    out_specs = (
        P(("grp", "gy"), "gx"),
        P(("grp", "gy"), "gx"),
        P(("grp", "gy"), "gx"),
        P(("grp", "gx"), "gy"),
    )
    return jax.shard_map(
        functools.partial(on_device, mesh.shape["gx"]),
        mesh=mesh, in_specs=in_specs, out_specs=out_specs, check_vma=False
    )
```

```python
import functools

import jax
import jax.numpy as jnp
from jax import lax
from jax.experimental import pallas as pl
from jax.experimental.pallas import tpu as pltpu
from jax.sharding import PartitionSpec as P

MESH = pl.DeviceIdType.MESH
F32 = jnp.float32
BF16 = jnp.bfloat16


def ring_place(n, me):
    if n > 8:
        return me
    up, side = me // 2, me % 2
    return (1 - side) * up + side * (n - 1 - up)


def ring_member(n, place):
    if n > 8:
        return place
    late = place // (n // 2)
    return (1 - late) * 2 * place + late * (2 * (n - 1 - place) + 1)


def terms_kernel(n, tiles, width, x_in, g_in, wg, wu, wd, hid, gt, ut, x_out, g_out,
                 xb, gb, wgu, wdb, a_own, a_got, b_own, b_got,
                 in_sem, wgu_sem, wd_sem, ring_send, ring_recv, sib_send, sib_recv,
                 part_send, part_recv, out_sem, credit):
    half = n // 2
    me, t = lax.axis_index("gx"), lax.axis_index("gy")
    sib = 1 - t
    place = ring_place(n, me)
    right = ring_member(n, lax.rem(place + 1, n))
    left = ring_member(n, lax.rem(place + n - 1, n))
    dl, dh = x_in.shape[-1], x_out.shape[-1]
    rows = 4 * xb.shape[-2]
    my_half = pl.ds(pl.multiple_of(t * dh, 128), dh)

    def cell(buf, j, whose, c):
        return buf.at[whose, c, :, pl.ds(pl.multiple_of(j * dl, 128), dl)]

    def own_in(arr, c):
        src, buf = ((x_in, xb), (g_in, gb))[arr]
        return pltpu.make_async_copy(src.at[c], cell(buf, me, t, c), in_sem.at[arr, c])

    for arr in range(2):
        for c in range(2):
            own_in(arr, c).start()

    barrier = pltpu.get_barrier_semaphore()
    pl.semaphore_signal(barrier, inc=1, device_id={"gx": left}, device_id_type=MESH)
    pl.semaphore_signal(barrier, inc=1, device_id={"gx": right}, device_id_type=MESH)
    pl.semaphore_signal(barrier, inc=1, device_id={"gy": sib}, device_id_type=MESH)
    pl.semaphore_wait(barrier, 3)

    def hop(arr, j, s, c, way):
        buf = (xb, gb)[arr]
        return pltpu.make_async_remote_copy(
            src_ref=cell(buf, j, t, c), dst_ref=cell(buf, j, t, c),
            send_sem=ring_send.at[arr, s - 1, c, way], recv_sem=ring_recv.at[arr, s - 1, c, way],
            device_id={"gx": (right, left)[way]}, device_id_type=MESH)

    def across(arr, j, c, whose):
        buf = (xb, gb)[arr]
        return pltpu.make_async_remote_copy(
            src_ref=cell(buf, j, whose, c), dst_ref=cell(buf, j, whose, c),
            send_sem=sib_send.at[arr, j % half, c], recv_sem=sib_recv.at[arr, j % half, c],
            device_id={"gy": sib}, device_id_type=MESH)

    def to_sibling(arr, j, c):
        @pl.when(j // half != t)
        def _():
            across(arr, j, c, t).start()

    def source(s, way):
        return ring_member(n, lax.rem(place + n + (s if way else -s), n))

    def begin(arr):
        for c in range(2):
            own_in(arr, c).wait()
            for way in range(2):
                hop(arr, me, 1, c, way).start()
            to_sibling(arr, me, c)

    def event(arr, e):
        s, c = 1 + e // 2, e % 2
        for way in range(2):
            j = source(s, way)
            hop(arr, j, s, c, way).wait_recv()

            @pl.when((s + 1 < half) | (c == way))
            def _():
                hop(arr, j, s + 1, c, way).start()

            to_sibling(arr, j, c)

    def last_event(arr):
        for way in range(2):
            j = source(half, way)
            hop(arr, j, half, way, way).wait_recv()
            to_sibling(arr, j, way)

    def from_sibling(arr):
        def one(k, carry):
            for c in range(2):
                across(arr, t * half + k, c, sib).wait_recv()
            return carry
        lax.fori_loop(0, half, one, 0)

    def weights(i, which):
        return pltpu.make_async_copy(
            (wg, wu)[which].at[:, pl.ds(pl.multiple_of(i * width, 128), width)],
            wgu.at[i % 2, which], wgu_sem.at[i % 2, which])

    def down(i):
        return pltpu.make_async_copy(
            wd.at[pl.ds(pl.multiple_of(i * width, 16), width), :], wdb.at[i], wd_sem.at[i])

    def part(which, i):
        src, dst = ((a_own, a_got), (b_own, b_got), (a_got, b_got))[which]
        return pltpu.make_async_remote_copy(
            src_ref=src.at[i], dst_ref=dst.at[i],
            send_sem=part_send.at[which, i], recv_sem=part_recv.at[which, i],
            device_id={"gy": sib}, device_id_type=MESH)

    begin(0)
    for i in range(min(2, tiles)):
        weights(i, 0).start()
        weights(i, 1).start()
    for i in range(tiles):
        down(i).start()

    def x_step(e, carry):
        event(0, e)
        return carry
    lax.fori_loop(0, 2 * (half - 2), x_step, 0)
    begin(1)
    lax.fori_loop(2 * (half - 2), 2 * (half - 1), x_step, 0)
    last_event(0)
    from_sibling(0)

    def first_half(i):
        at = pl.ds(pl.multiple_of(i * width, 128), width)
        part(0, i).wait()
        part(1, i).wait()
        gate = a_own[i] + a_got[i]
        up = b_own[i] + b_got[i]
        sig = 1.0 / (1.0 + jnp.exp(-gate))
        act = gate * sig
        hid[:, at] = (act * up).astype(BF16)
        a_own[i] = act
        b_own[i] = up * sig * (1.0 + gate * (1.0 - sig))

    def tile(i):
        for which, own in ((0, a_own), (1, b_own)):
            weights(i, which).wait()
            lhs = xb[:, :, :, my_half].reshape(rows, dh)
            own[i] = jnp.dot(lhs, wgu[i % 2, which], preferred_element_type=F32)
            part(which, i).start()

            @pl.when(i + 2 < tiles)
            def _():
                weights(i + 2, which).start()

        @pl.when(i > 0)
        def _():
            first_half(i - 1)

    def g_step(e, carry):
        event(1, e)

        @pl.when(e < tiles)
        def _():
            tile(e)
        return carry
    lax.fori_loop(0, 2 * (half - 1), g_step, 0)
    last_event(1)

    def rest(i, carry):
        tile(i)
        return carry
    lax.fori_loop(min(2 * (half - 1), tiles), tiles, rest, 0)
    first_half(tiles - 1)
    pl.semaphore_signal(credit, inc=1, device_id={"gy": sib}, device_id_type=MESH)
    from_sibling(1)

    def outs(arr):
        buf, out = ((xb, x_out), (gb, g_out))[arr]
        return pltpu.make_async_copy(buf.at[:, :, :, my_half], out, out_sem.at[arr])

    for arr in range(2):
        outs(arr).start()
    pl.semaphore_wait(credit, 1)

    def second_half(i):
        at = pl.ds(pl.multiple_of(i * width, 128), width)
        part(2, i).wait_recv()
        grad = a_got[i] + b_got[i]
        ut[:, at] = (grad * a_own[i]).astype(BF16)
        gt[:, at] = (grad * b_own[i]).astype(BF16)

    def grad_tile(i, carry):
        down(i).wait()
        lhs = gb[:, :, :, my_half].reshape(rows, dh)
        a_got[i] = lax.dot_general(lhs, wdb[i], (((1,), (1,)), ((), ())), preferred_element_type=F32)
        part(2, i).start()

        @pl.when(i > 0)
        def _():
            second_half(i - 1)
        return carry
    lax.fori_loop(0, tiles, grad_tile, 0)
    second_half(tiles - 1)

    def sent(i, carry):
        part(2, i).wait_send()
        return carry
    lax.fori_loop(0, tiles, sent, 0)

    for arr in range(2):
        outs(arr).wait()

        def crossed(k, carry):
            for c in range(2):
                across(arr, sib * half + k, c, t).wait_send()
            return carry
        lax.fori_loop(0, half, crossed, 0)

        def hopped(s, carry):
            for c in range(2):
                for way in range(2):
                    hop(arr, me, s, c, way).wait_send()
            return carry
        lax.fori_loop(1, half, hopped, 0)
        for way in range(2):
            hop(arr, me, half, way, way).wait_send()


def terms(n, inputs, out_grad, w_gate, w_up, w_down):
    tok, dl = inputs.shape
    dh, ff = w_gate.shape
    half = n // 2
    width = 256 if ff % 256 == 0 else ff
    tiles = ff // width
    anyspace = pl.BlockSpec(memory_space=pl.ANY)
    vmem = pl.BlockSpec(memory_space=pltpu.VMEM)
    quarter = tok // 2
    term = jax.ShapeDtypeStruct((2 * tok, ff), BF16)
    gathered = jax.ShapeDtypeStruct((2, 2, quarter, dh), BF16)
    dma = pltpu.SemaphoreType.DMA
    return pl.pallas_call(
        functools.partial(terms_kernel, n, tiles, width),
        out_shape=(term, term, term, gathered, gathered),
        in_specs=[anyspace] * 5,
        out_specs=(vmem, vmem, vmem, anyspace, anyspace),
        scratch_shapes=[
            pltpu.VMEM((2, 2, quarter, n * dl), BF16),
            pltpu.VMEM((2, 2, quarter, n * dl), BF16),
            pltpu.VMEM((2, 2, dh, width), BF16),
            pltpu.VMEM((tiles, width, dh), BF16),
            pltpu.VMEM((tiles, 2 * tok, width), F32),
            pltpu.VMEM((tiles, 2 * tok, width), F32),
            pltpu.VMEM((tiles, 2 * tok, width), F32),
            pltpu.VMEM((tiles, 2 * tok, width), F32),
            dma((2, 2)),
            dma((2, 2)),
            dma((tiles,)),
            dma((2, half, 2, 2)),
            dma((2, half, 2, 2)),
            dma((2, half, 2)),
            dma((2, half, 2)),
            dma((3, tiles)),
            dma((3, tiles)),
            dma((2,)),
            pltpu.SemaphoreType.REGULAR,
        ],
        compiler_params=pltpu.CompilerParams(
            collective_id=0, has_side_effects=True, vmem_limit_bytes=62 * 1024 * 1024),
        cost_estimate=pl.CostEstimate(
            flops=12 * tok * dh * ff, bytes_accessed=10 * dh * ff, transcendentals=2 * tok * ff),
    )(inputs.reshape(2, quarter, dl), out_grad.reshape(2, quarter, dl), w_gate, w_up, w_down)


def reduce_ring(n, blocks, me, work):
    half = n // 2
    members = [int(ring_member(n, p)) for p in range(n)]
    ways = [
        [(members[p], members[(p + 1) % n]) for p in range(n)],
        [(members[p], members[(p - 1) % n]) for p in range(n)],
    ]
    place = ring_place(n, me)
    got = [None, None]
    at_step = {(i + 1) * half // (len(work) + 1): i for i in range(len(work))}
    made = []
    for s in range(half):
        sends = []
        for way in range(2):
            d = half - s
            block = blocks(ring_member(n, (place + n + (-d if way else d)) % n))
            rows = block.shape[0]
            if s == 0:
                block = block[way * rows // 2:(way + 1) * rows // 2]
            elif s == 1:
                pad = (0, rows // 2) if way == 0 else (rows // 2, 0)
                block = block + jnp.pad(got[way].astype(F32), (pad, (0, 0)))
            else:
                block = block + got[way].astype(F32)
            sends.append(block.astype(BF16))
        if s in at_step:
            function, operand = work[at_step[s]]
            sends[0], sends[1], operand = lax.optimization_barrier((sends[0], sends[1], operand))
            product = function(operand)
        got = [lax.ppermute(sends[way], "gx", ways[way]) for way in range(2)]
        if s in at_step:
            got[0], got[1], product = lax.optimization_barrier((got[0], got[1], product))
            made.append(product)
    total = (blocks(me) + got[0].astype(F32) + got[1].astype(F32)).astype(BF16)
    return total, made


def on_device(n, inputs, out_grad, w_gate, w_up, w_down):
    tok, dl = inputs.shape
    dh, ff = w_gate.shape
    half = n // 2
    me, t = lax.axis_index("gx"), lax.axis_index("gy")
    hid, gt, ut, xh, gh = terms(n, inputs, out_grad, w_gate, w_up, w_down)
    xh, gh = xh.reshape(2 * tok, dh), gh.reshape(2 * tok, dh)

    def back(rows):
        a = lax.dynamic_slice_in_dim(gt, rows * tok, tok, 0)
        b = lax.dynamic_slice_in_dim(ut, rows * tok, tok, 0)
        nt = (((1,), (1,)), ((), ()))
        return lax.dot_general(a, w_gate, nt, preferred_element_type=F32) + lax.dot_general(
            b, w_up, nt, preferred_element_type=F32)

    theirs = lax.ppermute(back(1 - t).astype(BF16), "gy", [(0, 1), (1, 0)])
    mine = back(t)

    def blocks(q):
        at = (q % half) * dl
        own = lax.dynamic_slice_in_dim(mine, at, dl, 1)
        other = lax.dynamic_slice_in_dim(theirs, at, dl, 1).astype(F32)
        return jnp.where(q // half == t, own, other)

    def product(left):
        return lambda right: lax.dot_general(
            left, right, (((0,), (0,)), ((), ())), preferred_element_type=F32).astype(BF16)

    in_grad, (gate_grad, up_grad, down_grad) = reduce_ring(
        n, blocks, me, [(product(xh), gt), (product(xh), ut), (product(hid), gh)])
    return in_grad, gate_grad, up_grad, down_grad


def solution(mesh):
    in_specs = (
        P(("grp", "gy"), "gx"),
        P(("grp", "gy"), "gx"),
        P("gy", "gx"),
        P("gy", "gx"),
        P("gx", "gy"),
    )
    out_specs = (
        P(("grp", "gy"), "gx"),
        P(("grp", "gy"), "gx"),
        P(("grp", "gy"), "gx"),
        P(("grp", "gx"), "gy"),
    )
    return jax.shard_map(
        functools.partial(on_device, mesh.shape["gx"]),
        mesh=mesh, in_specs=in_specs, out_specs=out_specs, check_vma=False
    )
```
